32 devices in a mesh: rep: 2 (over y), gx: 4 (over z), gy: 4 (over x, core).
Axes of the slice: x: 2, y: 2, z: 4, core: 2. Of those that a mesh axis runs over, the one named last changes fastest.
Arguments:
- positions: float32 [8, 4, 3, 128], P(('rep', 'gx'), 'gy'), parts along dimension 0, as said below
- species: int32 [8, 4, 128], P(('rep', 'gx'), 'gy'), parts along dimension 0, may hold values from 0 to 5
- neighbours: int32 [8, 4, 8, 128], P(('rep', 'gx'), 'gy'), parts along dimension 0, may hold values from 0 to 287, as said below
- neighbour_count: int32 [8, 4, 128], P(('rep', 'gx'), 'gy'), parts along dimension 0, may hold values from 4 to 8
- face_rows: int32 [8, 4, 4, 32], P(('rep', 'gx'), 'gy'), parts along dimension 0, may hold values from 0 to 127, as said below
- corner_rows: int32 [8, 4, 4, 8], P(('rep', 'gx'), 'gy'), parts along dimension 0, may hold values from 0 to 127, as said below
- species_embed: float32 [6, 128], replicated, may hold values from -5 to 5
- atom_energy: float32 [6], replicated, may hold values from -4 to 4
- radial_in: float32 [2, 8, 64], replicated, may hold values from -4 to 4
- radial_out: float32 [2, 64, 512], replicated, may hold values from -1.5 to 1.5
- mixing: float32 [2, 3, 128, 128], replicated, may hold values from -0.5 to 0.5
- vector_mix: float32 [128, 128], replicated, may hold values from -0.5 to 0.5
- readout: float32 [2, 128], replicated, may hold values from -0.5 to 0.5
Outputs:
- node_energy: float32 [8, 4, 128], P(('rep', 'gx'), 'gy'), parts along dimension 0
- forces: float32 [8, 4, 3, 128], P(('rep', 'gx'), 'gy'), parts along dimension 0
The draws below stay inside these ranges and needn't reach their ends.
There are 2 independent parts, one for each index of `rep`. The reference program is written for one: setup_inputs(seed, part) draws one part's arguments, and reference() takes and returns one part's arrays. A program takes and returns all parts, laid end to end along the dimension named above; an argument that names none is the same for every part. Nothing has to cross between parts.
Inputs may be any that keep to these rules, and one draw needn't show every extreme that they name: `positions`: coordinates x and y lie in 0 to 17.6, z in 0 to 2.2 * 2; the atoms of one column's table, with the offsets added, are at least 0.5 apart. `neighbours`: the 8 slots of one atom name distinct rows of its column's table, never the atom itself. face_rows[x, y, f] holds 32 distinct atoms of column (x, y); they become face block f of the column at (x, y) minus the f-th face offset. corner_rows[x, y, c] holds 8 distinct atoms of column (x, y); they become corner block c of the column at (x, y) minus the c-th corner offset.
All inputs are finite; a program needn't handle non-finite values.
Results may differ from the reference program's by a relative error of at most 0.0003.
Values sent between devices are 32-bit elements; how exact they have to be, the bound alone decides.
A program may use at most 128 MiB of HBM per device.

```python
import math
import jax
import jax.numpy as jnp
import numpy as np
from jax import lax

C = 128
NB = 8
RH = 64
NSPEC = 6
A = 128
K = 8
N_GX = 4
N_GY = 4


spacing = 2.2


side_sites = 8


halo_planes = 2


reach_limit = 5


face_offsets = ((-1, 0), (1, 0), (0, -1), (0, 1))


corner_offsets = ((-1, -1), (1, -1), (-1, 1), (1, 1))


def lattice_order(key):
    column_keys = jax.random.split(key, N_GX * N_GY)
    permuted = jax.vmap(lambda column_key: jax.random.permutation(column_key, A))(column_keys)
    return permuted.reshape(N_GX, N_GY, A).astype(jnp.int32)


def plane_sites(offset):
    site_list = np.arange(A)
    lattice_x = site_list % side_sites
    lattice_y = site_list // side_sites % side_sites
    keep_site = np.ones(A, dtype=bool)
    if offset[0] == -1:
        keep_site = keep_site & (lattice_x >= side_sites - halo_planes)
    if offset[0] == 1:
        keep_site = keep_site & (lattice_x < halo_planes)
    if offset[1] == -1:
        keep_site = keep_site & (lattice_y >= side_sites - halo_planes)
    if offset[1] == 1:
        keep_site = keep_site & (lattice_y < halo_planes)
    return site_list[keep_site]


def ghost_coords():
    pieces = []
    plane = side_sites * side_sites
    for offset in face_offsets + corner_offsets:
        site_list = plane_sites(offset)
        pieces.append(np.stack([site_list % side_sites + side_sites * offset[0], site_list // side_sites % side_sites + side_sites * offset[1], site_list // plane], axis=1))
    return np.concatenate(pieces, axis=0).astype(np.int32)


def draw_positions(key, part):
    permuted = lattice_order(key)
    key = jax.random.fold_in(key, 17)
    plane = side_sites * side_sites
    lattice = jnp.stack([permuted % side_sites, permuted // side_sites % side_sites, permuted // plane], axis=2).astype(jnp.float32) + 0.5
    jitter = jnp.clip(0.12 * jax.random.normal(key, lattice.shape, jnp.float32), -0.3, 0.3)
    return (lattice + jitter) * spacing


def draw_neighbours(key, part):
    permuted = lattice_order(key)
    key = jax.random.fold_in(key, 11)
    plane = side_sites * side_sites
    local_coords = jnp.stack([permuted % side_sites, permuted // side_sites % side_sites, permuted // plane], axis=-1)
    ghost_table = jnp.asarray(ghost_coords())
    ghost_table = jnp.broadcast_to(ghost_table, (N_GX, N_GY) + ghost_table.shape)
    coords_table = jnp.concatenate([local_coords, ghost_table], axis=2)
    delta = coords_table[:, :, None, :, :] - local_coords[:, :, :, None, :]
    reach = jnp.sum(delta * delta, axis=-1)
    nearby = (reach > 0) & (reach <= reach_limit)
    table_rows = coords_table.shape[2]
    row_ids = jnp.arange(table_rows, dtype=jnp.int32)
    scores = jax.random.randint(key, reach.shape, 0, 65536, jnp.int32) * table_rows + row_ids
    scores = jnp.where(nearby, scores, -1 - row_ids)
    chosen = lax.top_k(scores, K)[1].astype(jnp.int32)
    return jnp.transpose(chosen, (0, 1, 3, 2))


def draw_neighbour_count(key, part):
    key = jax.random.fold_in(key, 13)
    count_key, full_key = jax.random.split(key)
    counts = jax.random.randint(count_key, (N_GX, N_GY, A), K // 2, K + 1, jnp.int32)
    full_atom = jax.random.randint(full_key, (N_GX, N_GY, 1), 0, A, jnp.int32)
    return jnp.where(jnp.arange(A, dtype=jnp.int32) == full_atom, K, counts).astype(jnp.int32)


def draw_face_rows(key, part):
    inverse = jnp.argsort(lattice_order(key), axis=-1).astype(jnp.int32)
    return jnp.stack([inverse[:, :, plane_sites(offset)] for offset in face_offsets], axis=2)


def draw_corner_rows(key, part):
    inverse = jnp.argsort(lattice_order(key), axis=-1).astype(jnp.int32)
    return jnp.stack([inverse[:, :, plane_sites(offset)] for offset in corner_offsets], axis=2)


def touch_ends(drawn, stream_key, least, high):
    longest = drawn.shape.index(max(drawn.shape))
    spots = []
    for shift in (0, 1):
        where = [jax.random.randint(jax.random.fold_in(stream_key, axis), (), 0, length) for axis, length in enumerate(drawn.shape)]
        where[longest] = (where[longest] + shift) % drawn.shape[longest]
        spots.append(tuple(where))
    return drawn.at[spots[0]].set(least).at[spots[1]].set(high)


def gaussian(rng, extent, scale, most, kind=jnp.bfloat16):
    array = jax.random.normal(rng, extent, jnp.float32) * scale
    return jnp.minimum(jnp.maximum(array, -most), most).astype(kind)


def setup_inputs(seed: int = 0, part: int = 0) -> dict:
    seeds = jax.random.split(jax.random.key(seed), 14)
    part_splits = jax.random.split(jax.random.fold_in(seeds[13], part), 14)
    positions = draw_positions(jax.random.fold_in(jax.random.fold_in(seeds[13], part), 71), part)
    species = touch_ends(jax.random.randint(part_splits[1], (N_GX, N_GY, A), 0, NSPEC), jax.random.fold_in(part_splits[1], 1), 0, NSPEC - 1).astype(jnp.int32)
    neighbours = draw_neighbours(jax.random.fold_in(jax.random.fold_in(seeds[13], part), 71), part)
    neighbour_count = draw_neighbour_count(jax.random.fold_in(jax.random.fold_in(seeds[13], part), 71), part)
    face_rows = draw_face_rows(jax.random.fold_in(jax.random.fold_in(seeds[13], part), 71), part)
    corner_rows = draw_corner_rows(jax.random.fold_in(jax.random.fold_in(seeds[13], part), 71), part)
    species_embed = gaussian(seeds[6], (NSPEC, C), 1.0, 5.0, jnp.float32)
    atom_energy = gaussian(seeds[7], (NSPEC,), 1.0, 4.0, jnp.float32)
    radial_in = gaussian(seeds[8], (2, NB, RH), 1.0, 4.0, jnp.float32)
    radial_out = gaussian(seeds[9], (2, RH, 4 * C), (RH // 4) ** -0.5, 1.5, jnp.float32)
    mixing = gaussian(seeds[10], (2, 3, C, C), C ** -0.5, 0.5, jnp.float32)
    vector_mix = gaussian(seeds[11], (C, C), C ** -0.5, 0.5, jnp.float32)
    readout = gaussian(seeds[12], (2, C), C ** -0.5, 0.5, jnp.float32)
    return dict(positions=positions, species=species, neighbours=neighbours, neighbour_count=neighbour_count, face_rows=face_rows, corner_rows=corner_rows, species_embed=species_embed, atom_energy=atom_energy, radial_in=radial_in, radial_out=radial_out, mixing=mixing, vector_mix=vector_mix, readout=readout)


cutoff = 5.0
column_width = 17.6
slot_group = 8
highest = lax.Precision.HIGHEST
face_offsets = ((-1, 0), (1, 0), (0, -1), (0, 1))
corner_offsets = ((-1, -1), (1, -1), (-1, 1), (1, 1))

def radial_basis(distance, count):
    orders = jnp.arange(1, count + 1, dtype=jnp.float32)
    scaled = distance / cutoff
    bessel = math.sqrt(2.0 / cutoff) * jnp.sin(orders[:, None] * jnp.pi * scaled[None, :]) / distance[None, :]
    inside = jnp.minimum(scaled, 1.0)
    envelope = 1.0 - 28.0 * inside ** 6 + 48.0 * inside ** 7 - 21.0 * inside ** 8
    return (bessel, envelope)

def interaction(position_table, feature_table, neighbours, live_mask, radial_in, radial_out):
    slot_count, atom_rows = neighbours.shape
    channels = feature_table.shape[0] // 4
    edge_scale = 1.0 / math.sqrt(slot_count)
    groups = slot_count // slot_group
    source_blocks = neighbours.reshape(groups, slot_group * atom_rows)
    mask_blocks = live_mask.reshape(groups, slot_group * atom_rows)
    centre = jnp.tile(position_table[:, :atom_rows], (1, slot_group))

    def accumulate(summed, inputs):
        source_rows, mask_row = inputs
        relative = jnp.take(position_table, source_rows, axis=1) - centre
        distance = jnp.sqrt(lax.optimization_barrier(jnp.sum(relative * relative, axis=0)))
        direction = relative / distance[None, :]
        bessel, envelope = radial_basis(distance, radial_in.shape[0])
        hidden = jax.nn.silu(jnp.einsum('nh,ne->he', radial_in, bessel, precision=highest))
        weights = jnp.einsum('hc,he->ce', radial_out, hidden, precision=highest)
        weights = (weights * (envelope * mask_row * edge_scale)[None, :]).reshape(4, channels, -1)
        source = jnp.take(feature_table, source_rows, axis=1).reshape(4, channels, -1)
        projected = direction[0][None] * source[1] + direction[1][None] * source[2] + direction[2][None] * source[3]
        scalar = weights[0] * source[0] + weights[1] * projected
        vector = weights[2][None] * direction[:, None, :] * source[0][None] + weights[3][None] * source[1:]
        message = jnp.concatenate([scalar[None], vector], axis=0).reshape(4, channels, slot_group, atom_rows)
        return (summed + lax.optimization_barrier(jnp.sum(message, axis=2)), None)
    initial = jnp.zeros((4, channels, atom_rows), jnp.float32)
    summed, unused = lax.scan(jax.checkpoint(accumulate), initial, (source_blocks, mask_blocks))
    return summed

def update(local_state, message, weights, vector_mix):
    channels = message.shape[1]
    current = local_state.reshape(4, channels, -1)
    scalar = jnp.einsum('cd,ca->da', weights[0], message[0], precision=highest)
    vector = jnp.einsum('cd,kca->kda', weights[1], message[1:], precision=highest)
    square = scalar * scalar + lax.optimization_barrier(jnp.sum(vector * vector, axis=0))
    new_scalar = current[0] + scalar + jnp.einsum('cd,ca->da', weights[2], square, precision=highest)
    if vector_mix is None:
        return new_scalar
    new_vector = current[1:] + vector + jnp.einsum('cd,kca->kda', vector_mix, scalar[None] * vector, precision=highest)
    return jnp.concatenate([new_scalar[None], new_vector], axis=0).reshape(4 * channels, -1)

def initial_features(species_row, species_embed):
    kind_count, channels = species_embed.shape
    onehot = (species_row == jnp.arange(kind_count, dtype=jnp.float32)[:, None]).astype(jnp.float32)
    scalar = jnp.einsum('sc,sr->cr', species_embed, onehot, precision=highest)
    return jnp.concatenate([scalar, jnp.zeros((3 * channels, scalar.shape[1]), jnp.float32)], axis=0)

def ghost_offsets(atom_rows, face_width, corner_width):
    shift_x = [jnp.zeros((atom_rows,), jnp.float32)]
    shift_y = [jnp.zeros((atom_rows,), jnp.float32)]
    for offset in face_offsets + corner_offsets:
        span_rows = face_width if offset in face_offsets else corner_width
        shift_x.append(jnp.full((span_rows,), offset[0] * column_width, jnp.float32))
        shift_y.append(jnp.full((span_rows,), offset[1] * column_width, jnp.float32))
    shift_x = jnp.concatenate(shift_x)
    shift_y = jnp.concatenate(shift_y)
    return jnp.stack([shift_x, shift_y, jnp.zeros_like(shift_x)])

def neighbour_tables(values, face_rows, corner_rows):
    pieces = [values]
    for offsets, row_lists in ((face_offsets, face_rows), (corner_offsets, corner_rows)):
        for which, offset in enumerate(offsets):
            source = jnp.roll(values, (-offset[0], -offset[1]), axis=(0, 1))
            chosen = jnp.roll(row_lists[:, :, which], (-offset[0], -offset[1]), axis=(0, 1))
            pieces.append(jnp.take_along_axis(source, chosen[:, :, None, :], axis=3))
    return jnp.concatenate(pieces, axis=3)

def reference(positions, species, neighbours, neighbour_count, face_rows, corner_rows, species_embed, atom_energy, radial_in, radial_out, mixing, vector_mix, readout):
    atom_rows = positions.shape[-1]
    slot_count = neighbours.shape[2]
    kind_count, channels = species_embed.shape
    column_count = N_GX * N_GY
    offsets = ghost_offsets(atom_rows, face_rows.shape[-1], corner_rows.shape[-1])
    species_code = species.astype(jnp.float32)[:, :, None, :]
    code_table = neighbour_tables(species_code, face_rows, corner_rows).reshape(column_count, 1, -1)
    live_slots = (jnp.arange(slot_count)[None, None, :, None] < neighbour_count[:, :, None, :]).astype(jnp.float32)
    live_slots = live_slots.reshape(column_count, slot_count, atom_rows)
    neighbour_flat = neighbours.reshape(column_count, slot_count, atom_rows)
    onehot_local = (species_code == jnp.arange(kind_count, dtype=jnp.float32)[:, None]).astype(jnp.float32)
    onehot_local = onehot_local.reshape(column_count, kind_count, atom_rows)

    def node_energies(coordinates):
        position_table = (neighbour_tables(coordinates, face_rows, corner_rows) + offsets).reshape(column_count, 3, -1)

        def first_layer(column):
            geometry, species_row, chosen, live_mask = column
            start_table = initial_features(species_row, species_embed)
            message = interaction(geometry, start_table, chosen, live_mask, radial_in[0], radial_out[0])
            return update(start_table[:, :atom_rows], message, mixing[0], vector_mix)
        layer_one = lax.map(first_layer, (position_table, code_table, neighbour_flat, live_slots))
        feature_table = neighbour_tables(layer_one.reshape(N_GX, N_GY, 4 * channels, atom_rows), face_rows, corner_rows)
        feature_table = feature_table.reshape(column_count, 4 * channels, -1)

        def second_layer(column):
            geometry, features, chosen, live_mask = column
            message = interaction(geometry, features, chosen, live_mask, radial_in[1], radial_out[1])
            return update(features[:, :atom_rows], message, mixing[1], None)
        layer_two = lax.map(second_layer, (position_table, feature_table, neighbour_flat, live_slots))
        energy = jnp.einsum('s,xsa->xa', atom_energy, onehot_local, precision=highest)
        energy = energy + jnp.einsum('c,xca->xa', readout[0], layer_one[:, :channels], precision=highest)
        energy = energy + jnp.einsum('c,xca->xa', readout[1], layer_two, precision=highest)
        return energy
    energy, pullback = jax.vjp(node_energies, positions)
    gradient = pullback(jnp.ones_like(energy))[0]
    return (energy.reshape(N_GX, N_GY, atom_rows), -gradient)
```

```python
import math

import jax
import jax.numpy as jnp
from jax import lax
from jax.experimental import pallas as pl
from jax.experimental.pallas import tpu as pltpu
from jax.sharding import PartitionSpec as P

cutoff = 5.0
column_width = 17.6
face_offsets = ((-1, 0), (1, 0), (0, -1), (0, 1))
corner_offsets = ((-1, -1), (1, -1), (-1, 1), (1, 1))
offsets = face_offsets + corner_offsets
f32 = jnp.float32
bf16 = jnp.bfloat16
MESH = pl.DeviceIdType.MESH
lane = 128
block = 32

sin_terms = [(-1) ** m * math.pi ** (2 * m + 1) / math.factorial(2 * m + 1) for m in range(8)]
cos_terms = [(-1) ** m * math.pi ** (2 * m) / math.factorial(2 * m) for m in range(8)]


def horner(terms, z):
    total = jnp.full_like(z, terms[-1])
    for term in terms[-2::-1]:
        total = total * z + term
    return total


def split(x):
    high = x.astype(bf16)
    return high, (x - high.astype(f32)).astype(bf16)


def thirds(x):
    high = x.astype(bf16).astype(f32)
    rest = x - high
    middle = rest.astype(bf16).astype(f32)
    return high, middle, rest - middle


def dot(a, b):
    return lax.dot_general(a, b, (((1,), (0,)), ((), ())), preferred_element_type=f32)


def dot_nt(a, b):
    return lax.dot_general(a, b, (((1,), (1,)), ((), ())), preferred_element_type=f32)


def dot3(a, b):
    return dot(a[0], b[0]) + (dot(a[0], b[1]) + dot(a[1], b[0]))


def fold(x):
    total = x[0:8]
    for start in range(8, x.shape[0], 8):
        total = total + x[start : start + 8]
    return total


def kernel(
    sizes,
    positions, species, neighbours, counts, faces, corners, embed, atom_energy,
    radial_in, radial_out, mixing, vector_mix, readout,
    energy_out, force_out,
    small, gather, picks, picks_t, mix, mix_t, rad_t, rad, w1, w2, h1, h2, unit,
    message, grad_message, dw_high, dw_low, dh_high, dh_low, du, tangent, hidden,
    state, start, layer, features, back,
    out0, in0, out1, in1, out2, in2, out3, in3, send_sem, recv_sem,
):
    count_x, count_y = sizes
    me_x, me_y = lax.axis_index("gx"), lax.axis_index("gy")
    atoms = positions.shape[3]
    slots = neighbours.shape[2]
    edges = slots * atoms
    kinds, channels = embed.shape
    orders, width = radial_in.shape[1:]
    face_width, corner_width = faces.shape[3], corners.shape[3]
    spans = []
    cursor = 0
    for offset in offsets:
        rows = face_width if offset in face_offsets else corner_width
        spans.append((cursor, rows))
        cursor += rows
    ghosts = cursor
    padded = 2 * lane

    def place(offset, sign):
        return {
            "gx": lax.rem(me_x + sign * offset[0] + count_x, count_x),
            "gy": lax.rem(me_y + sign * offset[1] + count_y, count_y),
        }

    barrier = pltpu.get_barrier_semaphore()
    for offset in offsets:
        pl.semaphore_signal(barrier, inc=1, device_id=place(offset, 1), device_id_type=MESH)

    def exchange(phase, source, target, sign):
        copies = []
        for which, offset in enumerate(offsets):
            first, rows = spans[which]
            copies.append(
                pltpu.make_async_remote_copy(
                    src_ref=source.at[pl.ds(first, rows)],
                    dst_ref=target.at[pl.ds(first, rows)],
                    send_sem=send_sem.at[phase, which],
                    recv_sem=recv_sem.at[phase, which],
                    device_id=place(offset, sign),
                    device_id_type=MESH,
                )
            )
        for copy in copies[4:] + copies[:4]:
            copy.start()
        return copies

    def arrive(copies):
        for copy in copies:
            copy.wait_recv()

    def pad_rows(x, rows):
        return jnp.concatenate([x, jnp.zeros((rows - x.shape[0], x.shape[1]), x.dtype)], axis=0)

    chosen = jnp.concatenate(
        [faces[0, 0, f : f + 1, :] for f in range(4)]
        + [corners[0, 0, c : c + 1, :] for c in range(4)]
        + [jnp.full((1, padded - ghosts), -1, jnp.int32)],
        axis=1,
    )
    onehot = (lax.broadcasted_iota(jnp.int32, (atoms, padded), 0) == chosen).astype(f32)
    picks_t[...] = onehot.astype(bf16)
    picks[...] = onehot.T[:ghosts].astype(bf16)

    code = species[0].astype(f32)
    small[...] = jnp.zeros_like(small)
    small[0:3, :] = positions[0, 0]
    small[3:4, :] = code
    own = small[0:8, :]
    own_parts = thirds(own)
    packet = 0.0
    for part in own_parts:
        packet = packet + dot_nt(picks[...], pad_rows(part, lane).astype(bf16))
    row = lax.broadcasted_iota(jnp.int32, (ghosts, lane), 0)
    column = lax.broadcasted_iota(jnp.int32, (ghosts, lane), 1)
    shift_x = jnp.zeros((ghosts, lane), f32)
    shift_y = jnp.zeros((ghosts, lane), f32)
    for which, offset in enumerate(offsets):
        first, rows = spans[which]
        inside = (row >= first) & (row < first + rows)
        shift_x = jnp.where(inside, offset[0] * column_width, shift_x)
        shift_y = jnp.where(inside, offset[1] * column_width, shift_y)
    out0[...] = packet + jnp.where(column == 0, shift_x, jnp.where(column == 1, shift_y, 0.0))
    pl.semaphore_wait(barrier, len(offsets))
    sent0 = exchange(0, out0, in0, -1)

    for k in range(slots):
        lanes = slice(k * lane, (k + 1) * lane)
        where = neighbours[0, 0, k : k + 1, :]
        hit = lax.broadcasted_iota(jnp.int32, (atoms + ghosts, lane), 0) == where
        gather[:, lanes] = hit.astype(f32).astype(bf16)
    local_pick = gather[0:atoms, :]
    ghost_pick = gather[atoms : atoms + ghosts, :]

    own_stack = pad_rows(jnp.concatenate(own_parts, axis=0), 32).astype(bf16)
    near = dot(own_stack, gather[0:atoms, :])

    for m in range(7):
        matrix = vector_mix[...] if m == 6 else mixing[m // 3, m % 3]
        mix[0, m], mix[1, m] = split(matrix)
        mix_t[0, m], mix_t[1, m] = split(matrix.T)

    def forward(m, x):
        parts = split(x)
        return dot3((mix_t[0, m], mix_t[1, m]), parts)

    def backward(m, x):
        parts = split(x)
        return dot3((mix[0, m], mix[1, m]), parts)

    both = jnp.concatenate([radial_out[0], radial_out[1]], axis=0)
    rad[0:128, :], rad[128:256, :] = split(both)
    turned = both.T
    turned_high = turned.astype(bf16).astype(f32)
    turned_low = turned - turned_high
    for l in range(2):
        c = slice(l * width, (l + 1) * width)
        rad_t[l] = jnp.concatenate(
            [turned_high[:, c], turned_high[:, c], turned_low[:, c]], axis=1
        ).astype(bf16)

    first_in = jnp.concatenate([radial_in[0], radial_in[1]], axis=1)
    first_high, first_middle, unused = thirds(first_in)
    first_mat = pad_rows(
        jnp.concatenate([first_high, first_high, first_middle], axis=0), lane
    ).T[:, :32].astype(bf16)

    small[8 : 8 + kinds, :] = embed[...]
    embed_mat = pad_rows(jnp.concatenate(thirds(small[8:16, :]), axis=0), lane).T[:, :32].astype(bf16)
    row8 = lax.broadcasted_iota(jnp.int32, (8, edges), 0)
    row8f = row8.astype(f32)

    def species_features(codes):
        hits = (row8f[:, : codes.shape[1]] == codes).astype(f32)
        return dot(embed_mat, pad_rows(jnp.concatenate([hits, hits, hits], axis=0), 32).astype(bf16))

    start[...] = species_features(code)
    readout_first = jnp.broadcast_to(readout[0:1, :], (lane, lane)).T
    readout_second = jnp.broadcast_to(readout[1:2, :], (lane, lane)).T
    pull_second = backward(5, readout_second)
    live = jnp.concatenate(
        [jnp.where(counts[0] > k, 1.0 / math.sqrt(slots), 0.0) for k in range(slots)], axis=1
    )
    centre = jnp.where(row8[:, :atoms] < 3, own, 0.0)
    centre = jnp.concatenate([centre] * slots, axis=1)

    arrive(sent0)
    arrived = pad_rows(in0[...], padded).T[0:8, :ghosts]
    arrived = pad_rows(jnp.concatenate(thirds(arrived), axis=0), 32).astype(bf16)
    far = dot(arrived, gather[atoms : atoms + ghosts, :])
    table = near + far
    table = (table[0:8] + table[8:16]) + table[16:24]
    codes = table[3:4, :]
    relative = jnp.where(row8 < 3, table - centre, 0.0)
    distance = jnp.sqrt(jnp.sum(relative * relative, axis=0, keepdims=True))
    inverse = 1.0 / distance
    direction = relative * inverse
    unit[...] = direction
    s = jnp.minimum(distance * (1.0 / cutoff), 1.0)
    s2 = s * s
    s5 = s2 * s2 * s
    envelope = 1.0 + s5 * s * (-28.0 + s * (48.0 - 21.0 * s))
    scale = envelope * live
    scale_slope = (-168.0 / cutoff) * s5 * (1.0 - s) * (1.0 - s) * live
    harmonic = row8f + 1.0
    turns = harmonic * s
    nearest = jnp.floor(turns + 0.5)
    y = turns - nearest
    half = nearest * 0.5
    sign = 1.0 - 4.0 * (half - jnp.floor(half))
    z = y * y
    sine = sign * y * horner(sin_terms, z)
    cosine = sign * horner(cos_terms, z)
    norm = math.sqrt(2.0 / cutoff) * inverse
    bessel = norm * sine
    bessel_slope = norm * ((math.pi / cutoff) * harmonic * cosine - sine * inverse)

    def hidden_input(x):
        high = x.astype(bf16).astype(f32)
        low = x - high
        stack = pad_rows(jnp.concatenate([high, low, high], axis=0), 32).astype(bf16)
        return dot(first_mat, stack)

    pre = hidden_input(bessel)
    pre_slope = hidden_input(bessel_slope)
    gate = 1.0 / (1.0 + jnp.exp(-pre))
    silu = pre * gate
    slope = gate * (1.0 + pre * (1.0 - gate))
    tangent[...] = scale_slope * silu + scale * slope * pre_slope
    scaled = scale * silu
    scaled_high, scaled_low = split(scaled)
    hidden[0] = jnp.concatenate(
        [scaled_high[:width], scaled_low[:width], scaled_high[:width]], axis=0
    )
    hidden[1] = jnp.concatenate(
        [scaled_high[width:], scaled_low[width:], scaled_high[width:]], axis=0
    )
    c1, c2, c3, c4 = channels, 2 * channels, 3 * channels, 4 * channels
    w1[0:c1, :] = dot(rad_t[0, 0:c1, :], hidden[0])
    w1[c1:c2, :] = dot(rad_t[0, c2:c3, :], hidden[0])
    h1[...] = species_features(codes)

    blocks = channels // block

    def units(lanes):
        return [unit[m : m + 1, lanes] for m in range(3)]

    def first_messages(step, carry):
        c = pl.multiple_of(step * block, block)
        total = [jnp.zeros((block, lane), f32) for m in range(4)]
        for k in range(slots):
            lanes = slice(k * lane, (k + 1) * lane)
            u = units(lanes)
            source = h1[pl.ds(c, block), lanes]
            total[0] = total[0] + w1[pl.ds(c, block), lanes] * source
            across = w1[pl.ds(c1 + c, block), lanes] * source
            for m in range(3):
                total[1 + m] = total[1 + m] + u[m] * across
        for m in range(4):
            message[pl.ds(m * c1 + c, block), :] = total[m]
        return carry

    lax.fori_loop(0, blocks, first_messages, 0)

    def side_by_side(x):
        return jnp.concatenate([x[c1:c2], x[c2:c3], x[c3:c4]], axis=1)

    def parts3(x):
        return x[:, 0:lane], x[:, lane : 2 * lane], x[:, 2 * lane : 3 * lane]

    scalar = forward(0, message[0:c1, :])
    vector = forward(1, side_by_side(message[...]))
    vx, vy, vz = parts3(vector)
    square = scalar * scalar + (vx * vx + vy * vy + vz * vz)
    scalar3 = jnp.concatenate([scalar, scalar, scalar], axis=1)
    new_scalar = start[...] + scalar + forward(2, square)
    new_vector = vector + forward(6, scalar3 * vector)
    state[:, 0:lane] = scalar
    state[:, lane : 4 * lane] = vector
    layer[0:c1, :] = new_scalar
    nx, ny, nz = parts3(new_vector)
    layer[c1:c2, :] = nx
    layer[c2:c3, :] = ny
    layer[c3:c4, :] = nz

    layer_high, layer_low = split(layer[...])
    features[:, 0:lane] = layer_high
    features[:, lane : 2 * lane] = layer_low
    out1[...] = dot_nt(picks[...], layer_high) + dot_nt(picks[...], layer_low)
    sent1 = exchange(1, out1, in1, -1)

    w2[...] = dot(rad_t[1], hidden[1])
    h2[...] = dot(
        features[...], jnp.concatenate([gather[0:atoms, :], gather[0:atoms, :]], axis=0)
    )
    arrive(sent1)
    far_features = pad_rows(in1[...], padded).T[:, :ghosts]
    far_high, far_low = split(far_features)
    h2[...] += dot(far_high, gather[atoms : atoms + ghosts, :]) + dot(
        far_low, gather[atoms : atoms + ghosts, :]
    )

    def second_messages(step, carry):
        c = pl.multiple_of(step * block, block)
        total = [jnp.zeros((block, lane), f32) for m in range(4)]
        for k in range(slots):
            lanes = slice(k * lane, (k + 1) * lane)
            u = units(lanes)
            w = [w2[pl.ds(m * c1 + c, block), lanes] for m in range(4)]
            h = [h2[pl.ds(m * c1 + c, block), lanes] for m in range(4)]
            along = u[0] * h[1] + u[1] * h[2] + u[2] * h[3]
            total[0] = total[0] + (w[0] * h[0] + w[1] * along)
            across = w[2] * h[0]
            for m in range(3):
                total[1 + m] = total[1 + m] + (u[m] * across + w[3] * h[1 + m])
        for m in range(4):
            message[pl.ds(m * c1 + c, block), :] = total[m]
        return carry

    lax.fori_loop(0, blocks, second_messages, 0)
    scalar2 = forward(3, message[0:c1, :])
    vector2 = forward(4, side_by_side(message[...]))
    grad_scalar2 = readout_second + 2.0 * scalar2 * pull_second
    grad_vector2 = 2.0 * vector2 * jnp.concatenate([pull_second] * 3, axis=1)

    def store_grad(first, second):
        grad_message[0:c1, :] = first
        sx, sy, sz = parts3(second)
        grad_message[c1:c2, :] = sx
        grad_message[c2:c3, :] = sy
        grad_message[c3:c4, :] = sz

    store_grad(backward(3, grad_scalar2), backward(4, grad_vector2))
    du[...] = jnp.zeros_like(du)

    def store_split(high, low, at, lanes, x):
        a, b = split(x)
        high[pl.ds(at, block), lanes] = a
        low[pl.ds(at, block), lanes] = b

    def second_grads(step, carry):
        c = pl.multiple_of(step * block, block)
        d = [grad_message[pl.ds(m * c1 + c, block), :] for m in range(4)]
        for k in range(slots):
            lanes = slice(k * lane, (k + 1) * lane)
            u = units(lanes)
            w = [w2[pl.ds(m * c1 + c, block), lanes] for m in range(4)]
            h = [h2[pl.ds(m * c1 + c, block), lanes] for m in range(4)]
            along = u[0] * h[1] + u[1] * h[2] + u[2] * h[3]
            turn = u[0] * d[1] + u[1] * d[2] + u[2] * d[3]
            store_split(dw_high, dw_low, c, lanes, d[0] * h[0])
            store_split(dw_high, dw_low, c1 + c, lanes, d[0] * along)
            store_split(dw_high, dw_low, c2 + c, lanes, turn * h[0])
            store_split(
                dw_high, dw_low, c3 + c, lanes, d[1] * h[1] + d[2] * h[2] + d[3] * h[3]
            )
            store_split(dh_high, dh_low, c, lanes, w[0] * d[0] + w[2] * turn)
            inward = w[1] * d[0]
            across = w[2] * h[0]
            for m in range(3):
                store_split(
                    dh_high, dh_low, (1 + m) * c1 + c, lanes, inward * u[m] + w[3] * d[1 + m]
                )
                du[m * 8 : m * 8 + 8, lanes] += fold(inward * h[1 + m] + across * d[1 + m])
        return carry

    lax.fori_loop(0, blocks, second_grads, 0)
    out2[...] = dot_nt(gather[atoms : atoms + ghosts, :], dh_high[...]) + dot_nt(
        gather[atoms : atoms + ghosts, :], dh_low[...]
    )
    sent2 = exchange(2, out2, in2, 1)

    back[...] = dot_nt(gather[0:atoms, :], dh_high[...]) + dot_nt(gather[0:atoms, :], dh_low[...])
    hidden_rows = slice(width, 2 * width)
    pulled = dot(rad[width : 2 * width, :], dw_high[...])
    pulled = pulled + dot(rad[width : 2 * width, :], dw_low[...])
    pulled = pulled + dot(rad[128 + width : 128 + 2 * width, :], dw_high[...])
    radial_grad = jnp.sum(pulled * tangent[hidden_rows, :], axis=0, keepdims=True)

    square2 = scalar2 * scalar2 + sum(p * p for p in parts3(vector2))
    final = layer[0:c1, :] + scalar2 + forward(5, square2)
    energy = jnp.sum(readout_first * layer[0:c1, :] + readout_second * final, axis=0, keepdims=True)
    for kind in range(kinds):
        energy = energy + jnp.where(code == float(kind), atom_energy[kind], 0.0)
    energy_out[0] = energy

    arrive(sent2)
    in2_high, in2_low = split(in2[...])
    picked = picks_t[:, :ghosts]
    total_back = back[...] + (dot(picked, in2_high) + dot(picked, in2_low))
    grad_state = total_back.T
    g0 = grad_state[0:c1] + (readout_first + readout_second)
    g1 = side_by_side(grad_state)
    scalar = state[:, 0:lane]
    vector = state[:, lane : 4 * lane]
    pull = backward(2, g0)
    cross = backward(6, g1)
    crossed = parts3(cross * vector)
    grad_scalar = g0 + 2.0 * scalar * pull + (crossed[0] + crossed[1] + crossed[2])
    grad_vector = (
        g1
        + 2.0 * vector * jnp.concatenate([pull] * 3, axis=1)
        + jnp.concatenate([scalar] * 3, axis=1) * cross
    )
    store_grad(backward(0, grad_scalar), backward(1, grad_vector))

    def first_grads(step, carry):
        c = pl.multiple_of(step * block, block)
        d = [grad_message[pl.ds(m * c1 + c, block), :] for m in range(4)]
        for k in range(slots):
            lanes = slice(k * lane, (k + 1) * lane)
            u = units(lanes)
            source = h1[pl.ds(c, block), lanes]
            turn = u[0] * d[1] + u[1] * d[2] + u[2] * d[3]
            store_split(dw_high, dw_low, c, lanes, d[0] * source)
            store_split(dw_high, dw_low, c1 + c, lanes, turn * source)
            across = w1[pl.ds(c1 + c, block), lanes] * source
            for m in range(3):
                du[m * 8 : m * 8 + 8, lanes] += fold(across * d[1 + m])
        return carry

    lax.fori_loop(0, blocks, first_grads, 0)
    rad_high = jnp.concatenate([rad[0:width, 0:c1], rad[0:width, c2:c3]], axis=1)
    rad_low = jnp.concatenate([rad[128 : 128 + width, 0:c1], rad[128 : 128 + width, c2:c3]], axis=1)
    pulled = dot(rad_high, dw_high[0:c2, :]) + dot(rad_high, dw_low[0:c2, :])
    pulled = pulled + dot(rad_low, dw_high[0:c2, :])
    radial_grad = radial_grad + jnp.sum(pulled * tangent[0:width, :], axis=0, keepdims=True)

    turn_grad = jnp.concatenate(
        [jnp.sum(du[m * 8 : m * 8 + 8, :], axis=0, keepdims=True) for m in range(3)]
        + [jnp.zeros((5, edges), f32)],
        axis=0,
    )
    direction = unit[...]
    outward = jnp.sum(direction * turn_grad, axis=0, keepdims=True)
    pair = (turn_grad - direction * outward) * inverse + direction * radial_grad
    pair_high, pair_low = split(pad_rows(pair, lane))
    out3[...] = dot_nt(gather[atoms : atoms + ghosts, :], pair_high) + dot_nt(
        gather[atoms : atoms + ghosts, :], pair_low
    )
    sent3 = exchange(3, out3, in3, 1)
    mine = dot_nt(gather[0:atoms, :], pair_high) + dot_nt(gather[0:atoms, :], pair_low)
    centred = pair[:, 0:lane]
    for k in range(1, slots):
        centred = centred + pair[:, k * lane : (k + 1) * lane]
    arrive(sent3)
    in3_high, in3_low = split(in3[...])
    mine = mine + (dot(picked, in3_high) + dot(picked, in3_low))
    force_out[0, 0] = (centred - mine.T[0:8])[0:3]
    for copies in (sent0, sent1, sent2, sent3):
        for copy in copies:
            copy.wait_send()


def solution(mesh):
    sizes = (mesh.shape["gx"], mesh.shape["gy"])

    def per_device(*args):
        positions, neighbours = args[0], args[2]
        atoms = positions.shape[3]
        slots = neighbours.shape[2]
        edges = slots * atoms
        kinds, channels = args[6].shape
        width = args[8].shape[2]
        ghosts = 4 * args[4].shape[3] + 4 * args[5].shape[3]
        wide = 4 * channels
        scratch = [
            pltpu.VMEM((16, lane), f32),
            pltpu.VMEM((atoms + ghosts, edges), bf16),
            pltpu.VMEM((ghosts, atoms), bf16),
            pltpu.VMEM((atoms, 2 * lane), bf16),
            pltpu.VMEM((2, 7, channels, channels), bf16),
            pltpu.VMEM((2, 7, channels, channels), bf16),
            pltpu.VMEM((2, wide, 3 * width), bf16),
            pltpu.VMEM((4 * width, wide), bf16),
            pltpu.VMEM((2 * channels, edges), f32),
            pltpu.VMEM((wide, edges), f32),
            pltpu.VMEM((channels, edges), f32),
            pltpu.VMEM((wide, edges), f32),
            pltpu.VMEM((8, edges), f32),
            pltpu.VMEM((wide, atoms), f32),
            pltpu.VMEM((wide, atoms), f32),
            pltpu.VMEM((wide, edges), bf16),
            pltpu.VMEM((wide, edges), bf16),
            pltpu.VMEM((wide, edges), bf16),
            pltpu.VMEM((wide, edges), bf16),
            pltpu.VMEM((24, edges), f32),
            pltpu.VMEM((2 * width, edges), f32),
            pltpu.VMEM((2, 3 * width, edges), bf16),
            pltpu.VMEM((channels, 4 * lane), f32),
            pltpu.VMEM((channels, atoms), f32),
            pltpu.VMEM((wide, atoms), f32),
            pltpu.VMEM((wide, 2 * lane), bf16),
            pltpu.VMEM((atoms, wide), f32),
        ]
        for columns in (lane, wide, wide, lane):
            scratch += [pltpu.VMEM((ghosts, columns), f32)] * 2
        scratch += [pltpu.SemaphoreType.DMA((4, 8)), pltpu.SemaphoreType.DMA((4, 8))]
        vmem = pl.BlockSpec(memory_space=pltpu.VMEM)
        specs = [vmem] * len(args)
        specs[7] = pl.BlockSpec(memory_space=pltpu.SMEM)

        def body(*refs):
            kernel(sizes, *refs)

        return pl.pallas_call(
            body,
            out_shape=(
                jax.ShapeDtypeStruct((1, 1, atoms), f32),
                jax.ShapeDtypeStruct(positions.shape, f32),
            ),
            in_specs=specs,
            out_specs=(vmem, vmem),
            scratch_shapes=scratch,
            compiler_params=pltpu.CompilerParams(
                collective_id=0, has_side_effects=True, vmem_limit_bytes=48 * 1024 * 1024
            ),
        )(*args)

    return jax.shard_map(
        per_device,
        mesh=mesh,
        in_specs=(
            P(("rep", "gx"), "gy", None, None),
            P(("rep", "gx"), "gy", None),
            P(("rep", "gx"), "gy", None, None),
            P(("rep", "gx"), "gy", None),
            P(("rep", "gx"), "gy", None, None),
            P(("rep", "gx"), "gy", None, None),
            P(),
            P(),
            P(),
            P(),
            P(),
            P(),
            P(),
        ),
        out_specs=(P(("rep", "gx"), "gy", None), P(("rep", "gx"), "gy", None, None)),
        check_vma=False,
    )
```

```python
import math

import jax
import jax.numpy as jnp
from jax import lax
from jax.experimental import pallas as pl
from jax.experimental.pallas import tpu as pltpu
from jax.sharding import PartitionSpec as P

cutoff = 5.0
column_width = 17.6
face_offsets = ((-1, 0), (1, 0), (0, -1), (0, 1))
corner_offsets = ((-1, -1), (1, -1), (-1, 1), (1, 1))
offsets = face_offsets + corner_offsets
f32 = jnp.float32
bf16 = jnp.bfloat16
MESH = pl.DeviceIdType.MESH
lane = 128
block = 32

sin_terms = [(-1) ** m * math.pi ** (2 * m + 1) / math.factorial(2 * m + 1) for m in range(8)]
cos_terms = [(-1) ** m * math.pi ** (2 * m) / math.factorial(2 * m) for m in range(8)]


def horner(terms, z):
    total = jnp.full_like(z, terms[-1])
    for term in terms[-2::-1]:
        total = total * z + term
    return total


def split(x):
    high = x.astype(bf16)
    return high, (x - high.astype(f32)).astype(bf16)


def thirds(x):
    high = x.astype(bf16).astype(f32)
    rest = x - high
    middle = rest.astype(bf16).astype(f32)
    return high, middle, rest - middle


def dot(a, b):
    return lax.dot_general(a, b, (((1,), (0,)), ((), ())), preferred_element_type=f32)


def dot_nt(a, b):
    return lax.dot_general(a, b, (((1,), (1,)), ((), ())), preferred_element_type=f32)


def dot3(a, b):
    return dot(a[0], b[0]) + (dot(a[0], b[1]) + dot(a[1], b[0]))


def fold(x):
    total = x[0:8]
    for start in range(8, x.shape[0], 8):
        total = total + x[start : start + 8]
    return total


def kernel(
    sizes,
    *refs,
):
    inputs, energy_out, force_out, landed = refs[:13], refs[13], refs[14], refs[15:28]
    (
    positions, species, neighbours, counts, faces, corners, embed, atom_energy,
    radial_in, radial_out, mixing, vector_mix, readout,
    ) = landed
    (
    small, gather, picks, picks_t, mix, mix_t, rad_t, rad, w1, w2, h1, h2, unit,
    message, grad_message, dw_high, dw_low, dh_high, dh_low, du, tangent, hidden,
    state, start, layer, features, back,
    out0, in0, out1, in1, out2, in2, out3, in3, send_sem, recv_sem, load_sem,
    ) = refs[28:]
    count_x, count_y = sizes
    me_x, me_y = lax.axis_index("gx"), lax.axis_index("gy")
    atoms = neighbours.shape[3]
    slots = neighbours.shape[2]
    edges = slots * atoms
    kinds, channels = embed.shape
    orders, width = radial_in.shape[1:]
    face_width, corner_width = faces.shape[3], corners.shape[3]
    spans = []
    cursor = 0
    for offset in offsets:
        rows = face_width if offset in face_offsets else corner_width
        spans.append((cursor, rows))
        cursor += rows
    ghosts = cursor
    padded = 2 * lane

    def place(offset, sign):
        return {
            "gx": lax.rem(me_x + sign * offset[0] + count_x, count_x),
            "gy": lax.rem(me_y + sign * offset[1] + count_y, count_y),
        }

    loads = [
        pltpu.make_async_copy(inputs[m], landed[m], load_sem.at[m]) for m in range(len(inputs))
    ]
    first_loads = (4, 5, 0, 1)
    later_loads = (2, 3, 9, 10, 11, 8, 6, 12, 7)
    for m in first_loads + later_loads:
        loads[m].start()
    barrier = pltpu.get_barrier_semaphore()
    for offset in offsets:
        pl.semaphore_signal(barrier, inc=1, device_id=place(offset, 1), device_id_type=MESH)

    def exchange(phase, source, target, sign):
        copies = []
        for which, offset in enumerate(offsets):
            first, rows = spans[which]
            copies.append(
                pltpu.make_async_remote_copy(
                    src_ref=source.at[pl.ds(first, rows)],
                    dst_ref=target.at[pl.ds(first, rows)],
                    send_sem=send_sem.at[phase, which],
                    recv_sem=recv_sem.at[phase, which],
                    device_id=place(offset, sign),
                    device_id_type=MESH,
                )
            )
        for copy in copies[4:] + copies[:4]:
            copy.start()
        return copies

    def arrive(copies):
        for copy in copies:
            copy.wait_recv()

    def pad_rows(x, rows):
        return jnp.concatenate([x, jnp.zeros((rows - x.shape[0], x.shape[1]), x.dtype)], axis=0)

    for m in first_loads:
        loads[m].wait()
    chosen = jnp.concatenate(
        [faces[0, 0, f : f + 1, :] for f in range(4)]
        + [corners[0, 0, c : c + 1, :] for c in range(4)]
        + [jnp.full((1, padded - ghosts), -1, jnp.int32)],
        axis=1,
    )
    onehot = (lax.broadcasted_iota(jnp.int32, (atoms, padded), 0) == chosen).astype(f32)
    picks_t[...] = onehot.astype(bf16)
    picks[...] = onehot.T[:ghosts].astype(bf16)

    code = species[0].astype(f32)
    small[...] = jnp.zeros_like(small)
    small[0:3, :] = positions[0, :, 0, :]
    small[3:4, :] = code
    own = small[0:8, :]
    own_parts = thirds(own)
    packet = 0.0
    for part in own_parts:
        packet = packet + dot_nt(picks[...], pad_rows(part, lane).astype(bf16))
    row = lax.broadcasted_iota(jnp.int32, (ghosts, lane), 0)
    column = lax.broadcasted_iota(jnp.int32, (ghosts, lane), 1)
    shift_x = jnp.zeros((ghosts, lane), f32)
    shift_y = jnp.zeros((ghosts, lane), f32)
    for which, offset in enumerate(offsets):
        first, rows = spans[which]
        inside = (row >= first) & (row < first + rows)
        shift_x = jnp.where(inside, offset[0] * column_width, shift_x)
        shift_y = jnp.where(inside, offset[1] * column_width, shift_y)
    out0[...] = packet + jnp.where(column == 0, shift_x, jnp.where(column == 1, shift_y, 0.0))
    pl.semaphore_wait(barrier, len(offsets))
    sent0 = exchange(0, out0, in0, -1)
    for m in later_loads:
        loads[m].wait()

    for k in range(slots):
        lanes = slice(k * lane, (k + 1) * lane)
        where = neighbours[0, 0, k : k + 1, :]
        hit = lax.broadcasted_iota(jnp.int32, (atoms + ghosts, lane), 0) == where
        gather[:, lanes] = hit.astype(f32).astype(bf16)
    local_pick = gather[0:atoms, :]
    ghost_pick = gather[atoms : atoms + ghosts, :]

    own_stack = pad_rows(jnp.concatenate(own_parts, axis=0), 32).astype(bf16)
    near = dot(own_stack, gather[0:atoms, :])

    for m in range(7):
        matrix = vector_mix[...] if m == 6 else mixing[m // 3, m % 3]
        mix[0, m], mix[1, m] = split(matrix)
        mix_t[0, m], mix_t[1, m] = split(matrix.T)

    def forward(m, x):
        parts = split(x)
        return dot3((mix_t[0, m], mix_t[1, m]), parts)

    def backward(m, x):
        parts = split(x)
        return dot3((mix[0, m], mix[1, m]), parts)

    both = jnp.concatenate([radial_out[0], radial_out[1]], axis=0)
    rad[0:128, :], rad[128:256, :] = split(both)
    turned = both.T
    turned_high = turned.astype(bf16).astype(f32)
    turned_low = turned - turned_high
    for l in range(2):
        c = slice(l * width, (l + 1) * width)
        rad_t[l] = jnp.concatenate(
            [turned_high[:, c], turned_high[:, c], turned_low[:, c]], axis=1
        ).astype(bf16)

    first_in = jnp.concatenate([radial_in[0], radial_in[1]], axis=1)
    first_high, first_middle, unused = thirds(first_in)
    first_mat = pad_rows(
        jnp.concatenate([first_high, first_high, first_middle], axis=0), lane
    ).T[:, :32].astype(bf16)

    small[8 : 8 + kinds, :] = embed[...]
    embed_mat = pad_rows(jnp.concatenate(thirds(small[8:16, :]), axis=0), lane).T[:, :32].astype(bf16)
    row8 = lax.broadcasted_iota(jnp.int32, (8, edges), 0)
    row8f = row8.astype(f32)

    def species_features(codes):
        hits = (row8f[:, : codes.shape[1]] == codes).astype(f32)
        return dot(embed_mat, pad_rows(jnp.concatenate([hits, hits, hits], axis=0), 32).astype(bf16))

    start[...] = species_features(code)
    readout_first = jnp.broadcast_to(readout[0:1, :], (lane, lane)).T
    readout_second = jnp.broadcast_to(readout[1:2, :], (lane, lane)).T
    pull_second = backward(5, readout_second)
    live = jnp.concatenate(
        [jnp.where(counts[0] > k, 1.0 / math.sqrt(slots), 0.0) for k in range(slots)], axis=1
    )
    centre = jnp.where(row8[:, :atoms] < 3, own, 0.0)
    centre = jnp.concatenate([centre] * slots, axis=1)

    arrive(sent0)
    arrived = pad_rows(in0[...], padded).T[0:8, :ghosts]
    arrived = pad_rows(jnp.concatenate(thirds(arrived), axis=0), 32).astype(bf16)
    far = dot(arrived, gather[atoms : atoms + ghosts, :])
    table = near + far
    table = (table[0:8] + table[8:16]) + table[16:24]
    codes = table[3:4, :]
    relative = jnp.where(row8 < 3, table - centre, 0.0)
    distance = jnp.sqrt(jnp.sum(relative * relative, axis=0, keepdims=True))
    inverse = 1.0 / distance
    direction = relative * inverse
    unit[...] = direction
    s = jnp.minimum(distance * (1.0 / cutoff), 1.0)
    s2 = s * s
    s5 = s2 * s2 * s
    envelope = 1.0 + s5 * s * (-28.0 + s * (48.0 - 21.0 * s))
    scale = envelope * live
    scale_slope = (-168.0 / cutoff) * s5 * (1.0 - s) * (1.0 - s) * live
    harmonic = row8f + 1.0
    turns = harmonic * s
    nearest = jnp.floor(turns + 0.5)
    y = turns - nearest
    half = nearest * 0.5
    sign = 1.0 - 4.0 * (half - jnp.floor(half))
    z = y * y
    sine = sign * y * horner(sin_terms, z)
    cosine = sign * horner(cos_terms, z)
    norm = math.sqrt(2.0 / cutoff) * inverse
    bessel = norm * sine
    bessel_slope = norm * ((math.pi / cutoff) * harmonic * cosine - sine * inverse)

    def hidden_input(x):
        high = x.astype(bf16).astype(f32)
        low = x - high
        stack = pad_rows(jnp.concatenate([high, low, high], axis=0), 32).astype(bf16)
        return dot(first_mat, stack)

    pre = hidden_input(bessel)
    pre_slope = hidden_input(bessel_slope)
    gate = 1.0 / (1.0 + jnp.exp(-pre))
    silu = pre * gate
    slope = gate * (1.0 + pre * (1.0 - gate))
    tangent[...] = scale_slope * silu + scale * slope * pre_slope
    scaled = scale * silu
    scaled_high, scaled_low = split(scaled)
    hidden[0] = jnp.concatenate(
        [scaled_high[:width], scaled_low[:width], scaled_high[:width]], axis=0
    )
    hidden[1] = jnp.concatenate(
        [scaled_high[width:], scaled_low[width:], scaled_high[width:]], axis=0
    )
    c1, c2, c3, c4 = channels, 2 * channels, 3 * channels, 4 * channels
    w1[0:c1, :] = dot(rad_t[0, 0:c1, :], hidden[0])
    w1[c1:c2, :] = dot(rad_t[0, c2:c3, :], hidden[0])
    h1[...] = species_features(codes)

    blocks = channels // block

    def units(lanes):
        return [unit[m : m + 1, lanes] for m in range(3)]

    def first_messages(step, carry):
        c = pl.multiple_of(step * block, block)
        total = [jnp.zeros((block, lane), f32) for m in range(4)]
        for k in range(slots):
            lanes = slice(k * lane, (k + 1) * lane)
            u = units(lanes)
            source = h1[pl.ds(c, block), lanes]
            total[0] = total[0] + w1[pl.ds(c, block), lanes] * source
            across = w1[pl.ds(c1 + c, block), lanes] * source
            for m in range(3):
                total[1 + m] = total[1 + m] + u[m] * across
        for m in range(4):
            message[pl.ds(m * c1 + c, block), :] = total[m]
        return carry

    lax.fori_loop(0, blocks, first_messages, 0)

    def side_by_side(x):
        return jnp.concatenate([x[c1:c2], x[c2:c3], x[c3:c4]], axis=1)

    def parts3(x):
        return x[:, 0:lane], x[:, lane : 2 * lane], x[:, 2 * lane : 3 * lane]

    scalar = forward(0, message[0:c1, :])
    vector = forward(1, side_by_side(message[...]))
    vx, vy, vz = parts3(vector)
    square = scalar * scalar + (vx * vx + vy * vy + vz * vz)
    scalar3 = jnp.concatenate([scalar, scalar, scalar], axis=1)
    new_scalar = start[...] + scalar + forward(2, square)
    new_vector = vector + forward(6, scalar3 * vector)
    state[:, 0:lane] = scalar
    state[:, lane : 4 * lane] = vector
    layer[0:c1, :] = new_scalar
    nx, ny, nz = parts3(new_vector)
    layer[c1:c2, :] = nx
    layer[c2:c3, :] = ny
    layer[c3:c4, :] = nz

    layer_high, layer_low = split(layer[...])
    features[:, 0:lane] = layer_high
    features[:, lane : 2 * lane] = layer_low
    out1[...] = dot_nt(picks[...], layer_high) + dot_nt(picks[...], layer_low)
    sent1 = exchange(1, out1, in1, -1)

    w2[...] = dot(rad_t[1], hidden[1])
    h2[...] = dot(
        features[...], jnp.concatenate([gather[0:atoms, :], gather[0:atoms, :]], axis=0)
    )
    arrive(sent1)
    far_features = pad_rows(in1[...], padded).T[:, :ghosts]
    far_high, far_low = split(far_features)
    h2[...] += dot(far_high, gather[atoms : atoms + ghosts, :]) + dot(
        far_low, gather[atoms : atoms + ghosts, :]
    )

    def second_messages(step, carry):
        c = pl.multiple_of(step * block, block)
        total = [jnp.zeros((block, lane), f32) for m in range(4)]
        for k in range(slots):
            lanes = slice(k * lane, (k + 1) * lane)
            u = units(lanes)
            w = [w2[pl.ds(m * c1 + c, block), lanes] for m in range(4)]
            h = [h2[pl.ds(m * c1 + c, block), lanes] for m in range(4)]
            along = u[0] * h[1] + u[1] * h[2] + u[2] * h[3]
            total[0] = total[0] + (w[0] * h[0] + w[1] * along)
            across = w[2] * h[0]
            for m in range(3):
                total[1 + m] = total[1 + m] + (u[m] * across + w[3] * h[1 + m])
        for m in range(4):
            message[pl.ds(m * c1 + c, block), :] = total[m]
        return carry

    lax.fori_loop(0, blocks, second_messages, 0)
    scalar2 = forward(3, message[0:c1, :])
    vector2 = forward(4, side_by_side(message[...]))
    grad_scalar2 = readout_second + 2.0 * scalar2 * pull_second
    grad_vector2 = 2.0 * vector2 * jnp.concatenate([pull_second] * 3, axis=1)

    def store_grad(first, second):
        grad_message[0:c1, :] = first
        sx, sy, sz = parts3(second)
        grad_message[c1:c2, :] = sx
        grad_message[c2:c3, :] = sy
        grad_message[c3:c4, :] = sz

    store_grad(backward(3, grad_scalar2), backward(4, grad_vector2))
    du[...] = jnp.zeros_like(du)

    def store_split(high, low, at, lanes, x):
        a, b = split(x)
        high[pl.ds(at, block), lanes] = a
        low[pl.ds(at, block), lanes] = b

    def second_grads(step, carry):
        c = pl.multiple_of(step * block, block)
        d = [grad_message[pl.ds(m * c1 + c, block), :] for m in range(4)]
        for k in range(slots):
            lanes = slice(k * lane, (k + 1) * lane)
            u = units(lanes)
            w = [w2[pl.ds(m * c1 + c, block), lanes] for m in range(4)]
            h = [h2[pl.ds(m * c1 + c, block), lanes] for m in range(4)]
            along = u[0] * h[1] + u[1] * h[2] + u[2] * h[3]
            turn = u[0] * d[1] + u[1] * d[2] + u[2] * d[3]
            store_split(dw_high, dw_low, c, lanes, d[0] * h[0])
            store_split(dw_high, dw_low, c1 + c, lanes, d[0] * along)
            store_split(dw_high, dw_low, c2 + c, lanes, turn * h[0])
            store_split(
                dw_high, dw_low, c3 + c, lanes, d[1] * h[1] + d[2] * h[2] + d[3] * h[3]
            )
            store_split(dh_high, dh_low, c, lanes, w[0] * d[0] + w[2] * turn)
            inward = w[1] * d[0]
            across = w[2] * h[0]
            for m in range(3):
                store_split(
                    dh_high, dh_low, (1 + m) * c1 + c, lanes, inward * u[m] + w[3] * d[1 + m]
                )
                du[m * 8 : m * 8 + 8, lanes] += fold(inward * h[1 + m] + across * d[1 + m])
        return carry

    lax.fori_loop(0, blocks, second_grads, 0)
    out2[...] = dot_nt(gather[atoms : atoms + ghosts, :], dh_high[...]) + dot_nt(
        gather[atoms : atoms + ghosts, :], dh_low[...]
    )
    sent2 = exchange(2, out2, in2, 1)

    back[...] = dot_nt(gather[0:atoms, :], dh_high[...]) + dot_nt(gather[0:atoms, :], dh_low[...])
    hidden_rows = slice(width, 2 * width)
    pulled = dot(rad[width : 2 * width, :], dw_high[...])
    pulled = pulled + dot(rad[width : 2 * width, :], dw_low[...])
    pulled = pulled + dot(rad[128 + width : 128 + 2 * width, :], dw_high[...])
    radial_grad = jnp.sum(pulled * tangent[hidden_rows, :], axis=0, keepdims=True)

    square2 = scalar2 * scalar2 + sum(p * p for p in parts3(vector2))
    final = layer[0:c1, :] + scalar2 + forward(5, square2)
    energy = jnp.sum(readout_first * layer[0:c1, :] + readout_second * final, axis=0, keepdims=True)
    for kind in range(kinds):
        energy = energy + jnp.where(code == float(kind), atom_energy[kind], 0.0)
    energy_out[0] = energy

    arrive(sent2)
    in2_high, in2_low = split(in2[...])
    picked = picks_t[:, :ghosts]
    total_back = back[...] + (dot(picked, in2_high) + dot(picked, in2_low))
    grad_state = total_back.T
    g0 = grad_state[0:c1] + (readout_first + readout_second)
    g1 = side_by_side(grad_state)
    scalar = state[:, 0:lane]
    vector = state[:, lane : 4 * lane]
    pull = backward(2, g0)
    cross = backward(6, g1)
    crossed = parts3(cross * vector)
    grad_scalar = g0 + 2.0 * scalar * pull + (crossed[0] + crossed[1] + crossed[2])
    grad_vector = (
        g1
        + 2.0 * vector * jnp.concatenate([pull] * 3, axis=1)
        + jnp.concatenate([scalar] * 3, axis=1) * cross
    )
    store_grad(backward(0, grad_scalar), backward(1, grad_vector))

    def first_grads(step, carry):
        c = pl.multiple_of(step * block, block)
        d = [grad_message[pl.ds(m * c1 + c, block), :] for m in range(4)]
        for k in range(slots):
            lanes = slice(k * lane, (k + 1) * lane)
            u = units(lanes)
            source = h1[pl.ds(c, block), lanes]
            turn = u[0] * d[1] + u[1] * d[2] + u[2] * d[3]
            store_split(dw_high, dw_low, c, lanes, d[0] * source)
            store_split(dw_high, dw_low, c1 + c, lanes, turn * source)
            across = w1[pl.ds(c1 + c, block), lanes] * source
            for m in range(3):
                du[m * 8 : m * 8 + 8, lanes] += fold(across * d[1 + m])
        return carry

    lax.fori_loop(0, blocks, first_grads, 0)
    rad_high = jnp.concatenate([rad[0:width, 0:c1], rad[0:width, c2:c3]], axis=1)
    rad_low = jnp.concatenate([rad[128 : 128 + width, 0:c1], rad[128 : 128 + width, c2:c3]], axis=1)
    pulled = dot(rad_high, dw_high[0:c2, :]) + dot(rad_high, dw_low[0:c2, :])
    pulled = pulled + dot(rad_low, dw_high[0:c2, :])
    radial_grad = radial_grad + jnp.sum(pulled * tangent[0:width, :], axis=0, keepdims=True)

    turn_grad = jnp.concatenate(
        [jnp.sum(du[m * 8 : m * 8 + 8, :], axis=0, keepdims=True) for m in range(3)]
        + [jnp.zeros((5, edges), f32)],
        axis=0,
    )
    direction = unit[...]
    outward = jnp.sum(direction * turn_grad, axis=0, keepdims=True)
    pair = (turn_grad - direction * outward) * inverse + direction * radial_grad
    pair_high, pair_low = split(pad_rows(pair, lane))
    out3[...] = dot_nt(gather[atoms : atoms + ghosts, :], pair_high) + dot_nt(
        gather[atoms : atoms + ghosts, :], pair_low
    )
    sent3 = exchange(3, out3, in3, 1)
    mine = dot_nt(gather[0:atoms, :], pair_high) + dot_nt(gather[0:atoms, :], pair_low)
    centred = pair[:, 0:lane]
    for k in range(1, slots):
        centred = centred + pair[:, k * lane : (k + 1) * lane]
    arrive(sent3)
    in3_high, in3_low = split(in3[...])
    mine = mine + (dot(picked, in3_high) + dot(picked, in3_low))
    force = centred - mine.T[0:8]
    for m in range(3):
        force_out[0, m] = force[m : m + 1, :]
    for copies in (sent0, sent1, sent2, sent3):
        for copy in copies:
            copy.wait_send()


def solution(mesh):
    sizes = (mesh.shape["gx"], mesh.shape["gy"])

    def per_device(*args):
        args = (jnp.transpose(args[0], (0, 2, 1, 3)),) + args[1:]
        neighbours = args[2]
        atoms = neighbours.shape[3]
        slots = neighbours.shape[2]
        edges = slots * atoms
        kinds, channels = args[6].shape
        width = args[8].shape[2]
        ghosts = 4 * args[4].shape[3] + 4 * args[5].shape[3]
        wide = 4 * channels
        scratch = [pltpu.VMEM(a.shape, a.dtype) for a in args]
        scratch[7] = pltpu.SMEM(args[7].shape, f32)
        scratch += [
            pltpu.VMEM((16, lane), f32),
            pltpu.VMEM((atoms + ghosts, edges), bf16),
            pltpu.VMEM((ghosts, atoms), bf16),
            pltpu.VMEM((atoms, 2 * lane), bf16),
            pltpu.VMEM((2, 7, channels, channels), bf16),
            pltpu.VMEM((2, 7, channels, channels), bf16),
            pltpu.VMEM((2, wide, 3 * width), bf16),
            pltpu.VMEM((4 * width, wide), bf16),
            pltpu.VMEM((2 * channels, edges), f32),
            pltpu.VMEM((wide, edges), f32),
            pltpu.VMEM((channels, edges), f32),
            pltpu.VMEM((wide, edges), f32),
            pltpu.VMEM((8, edges), f32),
            pltpu.VMEM((wide, atoms), f32),
            pltpu.VMEM((wide, atoms), f32),
            pltpu.VMEM((wide, edges), bf16),
            pltpu.VMEM((wide, edges), bf16),
            pltpu.VMEM((wide, edges), bf16),
            pltpu.VMEM((wide, edges), bf16),
            pltpu.VMEM((24, edges), f32),
            pltpu.VMEM((2 * width, edges), f32),
            pltpu.VMEM((2, 3 * width, edges), bf16),
            pltpu.VMEM((channels, 4 * lane), f32),
            pltpu.VMEM((channels, atoms), f32),
            pltpu.VMEM((wide, atoms), f32),
            pltpu.VMEM((wide, 2 * lane), bf16),
            pltpu.VMEM((atoms, wide), f32),
        ]
        for columns in (lane, wide, wide, lane):
            scratch += [pltpu.VMEM((ghosts, columns), f32)] * 2
        scratch += [pltpu.SemaphoreType.DMA((4, 8)), pltpu.SemaphoreType.DMA((4, 8))]
        scratch += [pltpu.SemaphoreType.DMA((len(args),))]
        vmem = pl.BlockSpec(memory_space=pltpu.VMEM)
        specs = [pl.BlockSpec(memory_space=pltpu.MemorySpace.HBM)] * len(args)

        def body(*refs):
            kernel(sizes, *refs)

        energy, force = pl.pallas_call(
            body,
            out_shape=(
                jax.ShapeDtypeStruct((1, 1, atoms), f32),
                jax.ShapeDtypeStruct(args[0].shape, f32),
            ),
            in_specs=specs,
            out_specs=(vmem, vmem),
            scratch_shapes=scratch,
            compiler_params=pltpu.CompilerParams(
                collective_id=0, has_side_effects=True, vmem_limit_bytes=64 * 1024 * 1024
            ),
        )(*args)
        return energy, jnp.transpose(force, (0, 2, 1, 3))

    return jax.shard_map(
        per_device,
        mesh=mesh,
        in_specs=(
            P(("rep", "gx"), "gy", None, None),
            P(("rep", "gx"), "gy", None),
            P(("rep", "gx"), "gy", None, None),
            P(("rep", "gx"), "gy", None),
            P(("rep", "gx"), "gy", None, None),
            P(("rep", "gx"), "gy", None, None),
            P(),
            P(),
            P(),
            P(),
            P(),
            P(),
            P(),
        ),
        out_specs=(P(("rep", "gx"), "gy", None), P(("rep", "gx"), "gy", None, None)),
        check_vma=False,
    )
```
